128 devices in a mesh: row: 16 (over x, z_hi, core), col: 8 (over y, z_lo).
Axes of the slice: x: 4, y: 4, z: 4 (z_hi: 2, z_lo: 2; z = z_hi * 2 + z_lo), core: 2. Of those that a mesh axis runs over, the one named last changes fastest.
Arguments:
- skew_matrix: float32 [16384, 16384], P('row', 'col'), may hold values from -80 to 80, as said below
- first_reflector: float32 [16384, 128], P('row'), may hold values from -0.05625 to 0.05625
- first_factor: float32 [128, 128], replicated, may hold values from -0.6 to 1.5, as said below
- second_reflector: float32 [16384, 128], P('row'), may hold values from -0.05625 to 0.05625
- second_factor: float32 [128, 128], replicated, may hold values from -0.6 to 1.5, as said below
- vectors: float32 [16384, 4096], P('row', 'col'), may hold values from -6 to 6
Outputs:
- updated_matrix: float32 [16384, 16384], P('row', 'col')
- back_vectors: float32 [16384, 4096], P('row', 'col')
The draws below stay inside these ranges and needn't reach their ends.
Inputs may be any that keep to these rules, and one draw needn't show every extreme that they name: skew_matrix is skew-symmetric: entry (i, j) equals minus entry (j, i) exactly. first_factor is upper triangular with a positive diagonal. second_factor is upper triangular with a positive diagonal.
All inputs are finite; a program needn't handle non-finite values.
Results may differ from the reference program's by a relative error of at most 0.000059.
Values sent between devices are 32-bit elements; how exact they have to be, the bound alone decides.
No kernel may reach another device: no remote copies, remote signals or barrier semaphores. Data moves between devices by JAX's collectives and lax.ppermute only.
A program may use at most 128 MiB of HBM per device.

```python
import jax
import jax.numpy as jnp
from jax import lax

N = 16384
NB = 128
K = 4096


def draw_skew_matrix(key, part):
    mkey = jax.random.fold_in(key, 3)
    base = jnp.clip(jax.random.normal(mkey, (N, N), jnp.float32), -6.0, 6.0)
    skew = (base - base.T) * 0.7071
    return skew


def factor_draw(key):
    diagonal = jax.random.uniform(jax.random.fold_in(key, 1), (NB,), jnp.float32, 0.5, 1.5)
    upper = jnp.clip(0.1 * jax.random.normal(jax.random.fold_in(key, 2), (NB, NB), jnp.float32), -0.6, 0.6)
    return jnp.triu(upper, 1) + jnp.diag(diagonal)


def draw_first_factor(key, part):
    return factor_draw(jax.random.fold_in(key, 11))


def draw_second_factor(key, part):
    return factor_draw(jax.random.fold_in(key, 12))


def level_of(stream_key, extent, cuts, smallest, high):
    loudness = 1.0
    for position, blocks in cuts:
        heights = jax.random.uniform(jax.random.fold_in(jax.random.fold_in(stream_key, 6), position), (blocks,), jnp.float32, smallest / len(cuts), high / len(cuts))
        loudness = loudness * jnp.repeat(jnp.exp(heights), extent[position] // blocks).reshape((-1,) + (1,) * (len(extent) - 1 - position))
    return loudness


def centred(stream_key, shape, scale, limit, cuts=(), held_as=jnp.bfloat16):
    entries = jax.random.normal(stream_key, shape, jnp.float32) * scale
    if len(cuts) > 0:
        entries = level_of(stream_key, shape, cuts, -0.22, 0.18) * entries
    return jnp.clip(entries, min=-limit, max=limit).astype(held_as)


def setup_inputs(seed: int = 0) -> dict:
    keys = jax.random.split(jax.random.key(seed), 7)
    return {
        "skew_matrix": draw_skew_matrix(jax.random.fold_in(keys[6], 71), 0),
        "first_reflector": centred(keys[1], (N, NB), (1.2 / N**0.5), 0.05625, ((0, 16),), jnp.float32),
        "first_factor": draw_first_factor(jax.random.fold_in(keys[6], 71), 0),
        "second_reflector": centred(keys[3], (N, NB), (1.2 / N**0.5), 0.05625, ((0, 16),), jnp.float32),
        "second_factor": draw_second_factor(jax.random.fold_in(keys[6], 71), 0),
        "vectors": centred(keys[5], (N, K), 1.0, 6.0, ((0, 16), (1, 8)), jnp.float32),
    }


def multiply(left, right):
    return jnp.dot(left, right, precision=lax.Precision.HIGHEST, preferred_element_type=jnp.float32)


def transform(matrix, reflector, factor):
    product = multiply(matrix, reflector)
    wide = multiply(product, factor)
    gram = multiply(reflector.T, product)
    correction = multiply(multiply(factor.T, gram), factor)
    fixed = wide - 0.5 * multiply(reflector, correction)
    left = jnp.concatenate([reflector, -fixed], axis=1)
    right = jnp.concatenate([fixed, reflector], axis=1)
    return matrix + multiply(left, right.T)


def back_apply(vectors, reflector, factor):
    sums = multiply(reflector.T, vectors)
    return vectors - multiply(reflector, multiply(factor, sums))


def reference(skew_matrix, first_reflector, first_factor, second_reflector, second_factor, vectors):
    inner = transform(skew_matrix, first_reflector, first_factor)
    updated_matrix = transform(inner, second_reflector, second_factor)
    middle = back_apply(vectors, second_reflector, second_factor)
    back_vectors = back_apply(middle, first_reflector, first_factor)
    return updated_matrix, back_vectors
```

```python
import jax
import jax.numpy as jnp
from jax import lax
from jax.sharding import PartitionSpec as P

HIGH = lax.Precision.HIGH
BOTH = ("row", "col")
PAIRS = [[2 * i, 2 * i + 1] for i in range(8)]
SAME_CORE = [[2 * i + k for i in range(8)] for k in range(2)]


def dot(left, right, dims=((1,), (0,)), precision=HIGH):
    return lax.dot_general(left, right, (dims, ((), ())), precision=precision, preferred_element_type=jnp.float32)


def small(left, right, dims=((1,), (0,))):
    return dot(left, right, dims, lax.Precision.HIGHEST)


def swap_cores(value):
    return lax.ppermute(value, "row", [(i, i ^ 1) for i in range(16)])


def fetch_map(offset, flip):
    pairs = []
    for x in range(4):
        for y in range(4):
            for zh in range(2):
                for zl in range(2):
                    for k in range(2):
                        xt, yt, zht, zlt = (y - offset - x) % 4, x, (zl + flip) % 2, zh
                        xt = (y - x - offset) % 4
                        pairs.append((((x * 2 + zh) * 2 + k) * 8 + y * 2 + zl, ((xt * 2 + zht) * 2 + k) * 8 + yt * 2 + zlt))
    return sorted(pairs)


def turn_map():
    return [((2 * j + k) * 8 + c, (2 * c + k) * 8 + j) for j in range(8) for k in range(2) for c in range(8)]


def exchange(value, axis, groups):
    return lax.all_to_all(value, axis, 0, 0, tiled=True, axis_index_groups=groups)


def copies(value, times):
    return jnp.broadcast_to(value[None], (times,) + value.shape).reshape((times * value.shape[0],) + value.shape[1:])


def shards(matrix, v1, f1, v2, f2, vectors):
    core = lax.axis_index("row") % 2
    col = lax.axis_index("col")
    half1 = lax.ppermute(v1, BOTH, fetch_map(0, 0))
    half2 = lax.ppermute(v2, BOTH, fetch_map(2, 1))
    own = jnp.concatenate([v1, v2], axis=1)

    part = -dot(matrix, own, ((0,), (0,)))
    cross = small(v1, v2, ((0,), (0,)))
    cross = jnp.concatenate([cross, jnp.zeros_like(cross)], axis=1)

    sums = dot(own, vectors, ((0,), (0,)))
    sums = lax.psum_scatter(sums, "row", scatter_dimension=0, tiled=True)
    sums = lax.all_gather(sums, "row", axis=0, tiled=True)

    rows = part.shape[0] // 2
    part = jnp.concatenate([part.reshape(2, rows, 256), cross.reshape(2, 64, 256)], axis=1)
    part = exchange(part, "row", PAIRS).sum(0)
    p_part, c_part = part[:rows].reshape(8, 128, 256), part[rows:].reshape(8, 8, 256)
    part = jnp.concatenate([p_part, c_part], axis=1)
    part = exchange(part, "row", SAME_CORE).sum(0)
    p_own, c_own = part[:128], part[128:]

    turned = lax.ppermute(p_own, BOTH, turn_map())
    p_rows = exchange(copies(turned[None], 8), "col", None).reshape(1024, 256)
    gram = dot(own, p_rows, ((0,), (0,)))
    gram = lax.dynamic_slice_in_dim(gram, col * 32, 32, 0)

    got = exchange(copies(jnp.concatenate([p_own, c_own, gram], axis=0)[None], 8), "row", SAME_CORE)
    half_gram = got[:, 136:].sum(0)
    mine = jnp.concatenate([got[:, :128].reshape(1024, 256), got[:, 128:136].reshape(64, 256), half_gram], axis=0)
    theirs = swap_cores(mine)
    half_v = jnp.concatenate([half1, half2], axis=1)
    other_v = swap_cores(half_v)

    def ordered(a, b):
        return jnp.concatenate([jnp.where(core == 0, a, b), jnp.where(core == 0, b, a)], axis=0)

    p_cols = ordered(mine[:1024], theirs[:1024])
    c = ordered(mine[1024:1088], theirs[1024:1088])[:, :128]
    v_cols = ordered(half_v, other_v)
    gram = mine[1088:] + theirs[1088:]
    gram = exchange(copies(gram[None], 8), "col", None).reshape(256, 256)

    zero = jnp.zeros_like(c)
    g11, g21, g22 = gram[:128, :128], gram[128:, :128], gram[128:, 128:]
    x1 = small(small(f1.T, g11), f1)
    x1c = small(x1, c)
    d = small(f1.T, g21.T) - 0.5 * small(x1.T, c) + 0.5 * x1c
    f1c = small(f1, c)
    g22 = g22 - small(g21, f1c) + small(c.T, d)
    x2 = small(small(f2.T, g22), f2)
    a_right = -small(f1c, f2)
    b_right = small(d, f2)
    a = jnp.concatenate([jnp.concatenate([f1, a_right], 1), jnp.concatenate([zero, f2], 1)], 0)
    b = jnp.concatenate([jnp.concatenate([-0.5 * x1, b_right], 1), jnp.concatenate([zero, -0.5 * x2], 1)], 0)

    left = jnp.concatenate([dot(own, a, ((1,), (1,))), -dot(p_rows, a) - dot(own, b - b.T)], axis=1)
    right = jnp.concatenate([p_cols, v_cols], axis=1)
    updated = matrix + dot(left, right, ((1,), (1,)))

    t2 = small(f2, sums[128:])
    t1 = small(f1, sums[:128] - small(c, t2))
    back = vectors - dot(own, jnp.concatenate([t1, t2], axis=0))
    return updated, back


def solution(mesh):
    in_specs = (P("row", "col"), P("row", None), P(), P("row", None), P(), P("row", "col"))
    out_specs = (P("row", "col"), P("row", "col"))
    return jax.shard_map(shards, mesh=mesh, in_specs=in_specs, out_specs=out_specs, check_vma=False)
```

```python
import jax
import jax.numpy as jnp
from jax import lax
from jax.experimental import pallas as pl
from jax.experimental.pallas import tpu as pltpu
from jax.sharding import PartitionSpec as P

HIGH = lax.Precision.HIGH
BOTH = ("row", "col")
SAME_CORE = [[2 * i + k for i in range(8)] for k in range(2)]
F32 = jnp.float32
BF16 = jnp.bfloat16


def dot(left, right, dims=((1,), (0,)), precision=HIGH):
    return lax.dot_general(left, right, (dims, ((), ())), precision=precision, preferred_element_type=F32)


def small(left, right, dims=((1,), (0,))):
    return dot(left, right, dims, lax.Precision.HIGHEST)


def split(value):
    high = value.astype(BF16)
    return high, (value - high.astype(F32)).astype(BF16)


def mxu(left, right):
    return jnp.dot(left, right, preferred_element_type=F32)


def swap_cores(value):
    return lax.ppermute(value, "row", [(i, i ^ 1) for i in range(16)])


def fetch_map(offset, flip):
    pairs = []
    for x in range(4):
        for y in range(4):
            for zh in range(2):
                for zl in range(2):
                    for k in range(2):
                        xt, yt, zht, zlt = (y - x - offset) % 4, x, (zl + flip) % 2, zh
                        pairs.append((((x * 2 + zh) * 2 + k) * 8 + y * 2 + zl, ((xt * 2 + zht) * 2 + k) * 8 + yt * 2 + zlt))
    return sorted(pairs)


def turn_map():
    return [((2 * j + k) * 8 + c, (2 * c + k) * 8 + j) for j in range(8) for k in range(2) for c in range(8)]


def exchange(value, axis, groups):
    return lax.all_to_all(value, axis, 0, 0, axis_index_groups=groups, tiled=True)


def copies(value, times):
    return jnp.broadcast_to(value[None], (times,) + value.shape)


def half_kernel(which_ref, turned_ref, matrix_ref, out_ref, both_ref):
    @pl.when(pl.program_id(0) == 0)
    def _():
        high, low = split(-turned_ref[...])
        both_ref[:256] = high
        both_ref[256:] = low

    high, low = split(matrix_ref[...])
    first = mxu(both_ref[...], high)
    total = first[:256] + first[256:] + mxu(both_ref[:256], low)
    out_ref[0] = total[:, :128]
    out_ref[1] = total[:, 128:]


def half_product(which, turned, matrix):
    depth = matrix.shape[0]
    return pl.pallas_call(
        half_kernel,
        grid_spec=pltpu.PrefetchScalarGridSpec(
            num_scalar_prefetch=1,
            grid=(4,),
            in_specs=[
                pl.BlockSpec((256, depth), lambda i, which: (0, 0)),
                pl.BlockSpec((depth, 256), lambda i, which: (0, which[0] * 4 + i)),
            ],
            out_specs=pl.BlockSpec((2, 256, 128), lambda i, which: (i, 0, 0)),
            scratch_shapes=[pltpu.VMEM((512, depth), BF16)],
        ),
        out_shape=jax.ShapeDtypeStruct((8, 256, 128), F32),
        compiler_params=pltpu.CompilerParams(vmem_limit_bytes=32 * 2**20),
        cost_estimate=pl.CostEstimate(flops=3 * 2 * 256 * depth * 1024, bytes_accessed=4 * depth * 1024 + 2**20, transcendentals=0),
    )(which, turned, matrix)


def add_kernel(left_ref, right_ref, base_ref, out_ref, wide_ref):
    @pl.when(pl.program_id(0) == 0)
    def _():
        high, low = split(left_ref[...])
        wide_ref[:, :256] = high
        wide_ref[:, 256:512] = low

    high, low = split(jnp.concatenate([right_ref[0], right_ref[1]], axis=1))
    total = mxu(wide_ref[:, :256], high) + mxu(wide_ref[:, 256:], high) + mxu(wide_ref[:, :256], low)
    out_ref[...] = base_ref[...] + total


def add_product(left, right, base):
    rows, cols = base.shape
    return pl.pallas_call(
        add_kernel,
        grid=(cols // 256,),
        in_specs=[
            pl.BlockSpec((rows, 256), lambda i: (0, 0)),
            pl.BlockSpec((2, 256, 128), lambda i: (i, 0, 0)),
            pl.BlockSpec((rows, 256), lambda i: (0, i)),
        ],
        out_specs=pl.BlockSpec((rows, 256), lambda i: (0, i)),
        scratch_shapes=[pltpu.VMEM((rows, 512), BF16)],
        out_shape=jax.ShapeDtypeStruct((rows, cols), F32),
        compiler_params=pltpu.CompilerParams(vmem_limit_bytes=32 * 2**20),
        cost_estimate=pl.CostEstimate(flops=3 * 2 * rows * cols * 256, bytes_accessed=8 * rows * cols, transcendentals=0),
    )(left, right, base)


def shards(matrix, v1, f1, v2, f2, vectors):
    core = lax.axis_index("row") % 2
    chip = lax.axis_index("row") // 2
    col = lax.axis_index("col")

    def of_core(value):
        value = value.reshape((2, value.shape[0] // 2) + value.shape[1:])
        return value[core], value[1 - core]

    def ordered(mine, theirs):
        return jnp.concatenate([jnp.where(core == 0, mine, theirs), jnp.where(core == 0, theirs, mine)], axis=0)

    half1 = lax.ppermute(v1, BOTH, fetch_map(0, 0))
    half2 = lax.ppermute(v2, BOTH, fetch_map(2, 1))
    own = jnp.concatenate([v1, v2], axis=1)
    turned = own.T

    away = half_product((1 - core)[None], turned, matrix)
    came = swap_cores(away)
    kept = half_product(core[None], turned, matrix)

    sums = dot(turned, vectors).reshape(1024, 128)
    sums_kept, sums_away = of_core(sums)
    cross = dot(v1, v2, ((0,), (0,)))
    side = swap_cores(jnp.concatenate([sums_away, cross], axis=0))
    sums_kept = (sums_kept + side[:512]).reshape(8, 64, 128)
    cross = (cross + side[512:]).reshape(8, 16, 128)

    packed = jnp.concatenate([kept + came, sums_kept, cross], axis=1)
    packed = exchange(packed, "row", SAME_CORE).sum(0)

    over = lax.ppermute(packed[:256].T, BOTH, turn_map())
    got = exchange(copies(packed, 8), "row", SAME_CORE)
    half_p = got[:, :256]
    half_v = jnp.concatenate([half1, half2], axis=1)
    gram = dot(
        lax.dynamic_slice_in_dim(half_p, chip * 32, 32, 1).transpose(1, 0, 2).reshape(32, 1024),
        half_v,
    )
    p_rows = exchange(copies(jnp.concatenate([over, gram], axis=0), 8), "col", None)
    gram = p_rows[:, 128:].sum(0)
    p_rows = p_rows[:, :128].reshape(1024, 256)
    gram = gram + swap_cores(gram)
    gram = exchange(copies(gram, 8), "row", SAME_CORE).reshape(256, 256)

    p_cols = ordered(half_p, swap_cores(half_p))
    v_cols = ordered(half_v, swap_cores(half_v))
    half_s = got[:, 256:320].reshape(512, 128)
    sums = ordered(half_s, swap_cores(half_s)).reshape(256, 512)
    cross = got[:, 320:].reshape(128, 128)
    a_right = -small(small(f1, cross), f2)
    factor = jnp.concatenate(
        [jnp.concatenate([f1, a_right], axis=1), jnp.concatenate([jnp.zeros_like(f2), f2], axis=1)], axis=0
    )
    back = vectors - dot(own, dot(factor, sums))
    y_rows = dot(own, factor, ((1,), (1,)))
    y_cols = dot(factor, v_cols, ((1,), (1,))).reshape(256, 16, 128).transpose(1, 0, 2)

    inner = add_product(y_rows, p_cols, matrix)
    updated = add_product(-p_rows - dot(y_rows, gram), y_cols, inner)
    return updated, back


def solution(mesh):
    in_specs = (P("row", "col"), P("row", None), P(), P("row", None), P(), P("row", "col"))
    out_specs = (P("row", "col"), P("row", "col"))
    return jax.shard_map(shards, mesh=mesh, in_specs=in_specs, out_specs=out_specs, check_vma=False)
```

```python
import jax
import jax.numpy as jnp
from jax import lax
from jax.experimental import pallas as pl
from jax.experimental.pallas import tpu as pltpu
from jax.sharding import PartitionSpec as P

HIGH = lax.Precision.HIGH
BOTH = ("row", "col")
SAME_CORE = [[2 * i + k for i in range(8)] for k in range(2)]
F32 = jnp.float32
BF16 = jnp.bfloat16
WIDE = 512


def dot(left, right, dims=((1,), (0,)), precision=HIGH):
    return lax.dot_general(left, right, (dims, ((), ())), precision=precision, preferred_element_type=F32)


def small(left, right, dims=((1,), (0,))):
    return dot(left, right, dims, lax.Precision.HIGHEST)


def split(value):
    high = value.astype(BF16)
    return high, (value - high.astype(F32)).astype(BF16)


def mxu(left, right):
    return jnp.dot(left, right, preferred_element_type=F32)


def three(left, right):
    left_high, left_low = split(left)
    right_high, right_low = split(right)
    return mxu(left_high, right_high) + mxu(left_low, right_high) + mxu(left_high, right_low)


def row_swap(value, mask):
    return lax.ppermute(value, "row", [(i, i ^ mask) for i in range(16)])


def turn_map():
    return [((2 * j + k) * 8 + c, (2 * c + k) * 8 + j) for j in range(8) for k in range(2) for c in range(8)]


def exchange(value, axis, groups):
    return lax.all_to_all(value, axis, 0, 0, axis_index_groups=groups, tiled=True)


def copies(value, times):
    return jnp.broadcast_to(value[None], (times,) + value.shape)


def params(mebibytes):
    return pltpu.CompilerParams(vmem_limit_bytes=mebibytes * 2**20)


def cost(flops, bytes_accessed):
    return pl.CostEstimate(flops=flops, bytes_accessed=bytes_accessed, transcendentals=0)


def chunk_products(both_ref, matrix_ref, out_ref):
    high, low = split(matrix_ref[...])
    first = mxu(both_ref[...], high)
    total = -(first[:256] + first[256:] + mxu(both_ref[:256], low))
    for side in range(total.shape[1] // 128):
        out_ref[side] = total[:, side * 128 : side * 128 + 128]


def away_kernel(which_ref, v1_ref, v2_ref, matrix_ref, out_ref, both_ref):
    @pl.when(pl.program_id(0) == 0)
    def _():
        high, low = split(v1_ref[...].T)
        both_ref[0:128] = high
        both_ref[256:384] = low
        high, low = split(v2_ref[...].T)
        both_ref[128:256] = high
        both_ref[384:512] = low

    chunk_products(both_ref, matrix_ref, out_ref)


def kept_kernel(which_ref, both_ref, matrix_ref, out_ref):
    chunk_products(both_ref, matrix_ref, out_ref)


def half_product(kernel, which, sides, side_specs, matrix, more_shapes, more_specs):
    depth = matrix.shape[0]
    return pl.pallas_call(
        kernel,
        grid_spec=pltpu.PrefetchScalarGridSpec(
            num_scalar_prefetch=1,
            grid=(1024 // WIDE,),
            in_specs=side_specs
            + [pl.BlockSpec((depth, WIDE), lambda i, which: (0, which[0] * (1024 // WIDE) + i))],
            out_specs=[pl.BlockSpec((WIDE // 128, 256, 128), lambda i, which: (i, 0, 0))] + more_specs,
        ),
        out_shape=[jax.ShapeDtypeStruct((8, 256, 128), F32)] + more_shapes,
        compiler_params=params(58),
        cost_estimate=cost(3 * 2 * 256 * depth * 1024, 4 * depth * 1024 + 2**21),
    )(which, *sides, matrix)


def away_product(which, v1, v2, matrix):
    depth = matrix.shape[0]
    return half_product(
        away_kernel,
        which,
        (v1, v2),
        [pl.BlockSpec((depth, 128), lambda i, which: (0, 0))] * 2,
        matrix,
        [jax.ShapeDtypeStruct((512, depth), BF16)],
        [pl.BlockSpec((512, depth), lambda i, which: (0, 0))],
    )


def kept_product(which, both, matrix):
    depth = matrix.shape[0]
    spec = pl.BlockSpec((512, depth), lambda i, which: (0, 0))
    return half_product(kept_kernel, which, (both,), [spec], matrix, [], [])[0]


def side_kernel(core_ref, both_ref, v2_ref, vectors_ref, away_ref, kept_ref, sums_ref):
    high, low = split(vectors_ref[...])
    sums_ref[...] = mxu(both_ref[:256], high) + mxu(both_ref[256:], high) + mxu(both_ref[:256], low)
    high, low = split(v2_ref[...])
    cross = mxu(both_ref[:128], high) + mxu(both_ref[256:384], high) + mxu(both_ref[:128], low)
    for out_ref, half in ((kept_ref, core_ref[0]), (away_ref, 1 - core_ref[0])):
        for j in range(8):
            rows = pl.ds(pl.multiple_of(half * 128 + j * 16, 16), 16)
            for block in range(4):
                out_ref[j, 16 * block : 16 * block + 16] = sums_ref[rows, block * 128 : block * 128 + 128]
            out_ref[j, 64:] = cross[j * 16 : j * 16 + 16]


def side_products(core, both, v2, vectors):
    return pl.pallas_call(
        side_kernel,
        in_specs=[pl.BlockSpec(memory_space=pltpu.SMEM)] + [pl.BlockSpec(memory_space=pltpu.VMEM)] * 3,
        out_shape=[jax.ShapeDtypeStruct((8, 80, 128), F32)] * 2,
        scratch_shapes=[pltpu.VMEM((256, 512), F32)],
        compiler_params=params(16),
        cost_estimate=cost(3 * 2 * 256 * 1024 * 640, 2**22),
    )(core, both, v2, vectors)


def pack_kernel(kept_ref, came_ref, side_kept_ref, side_came_ref, out_ref):
    out_ref[:, :256] = kept_ref[...] + came_ref[...]
    out_ref[:, 256:] = side_kept_ref[...] + side_came_ref[...]


def pack(*parts):
    return pl.pallas_call(
        pack_kernel,
        out_shape=jax.ShapeDtypeStruct((8, 336, 128), F32),
        compiler_params=params(16),
        cost_estimate=cost(2**19, 2**22),
    )(*parts)


def chunk_kernel(parts_ref, v_ref, out_ref, rows_ref):
    total = parts_ref[0]
    for j in range(1, 8):
        total = total + parts_ref[j]
    rows_ref[...] = total[:256].T
    gram = three(total[:256], v_ref[...])
    for j in range(8):
        out_ref[j, :336] = total
        out_ref[j, 336:368] = gram[j * 32 : j * 32 + 32, :128]
        out_ref[j, 368:400] = gram[j * 32 : j * 32 + 32, 128:]
        out_ref[j, 400:528] = v_ref[:, :128]
        out_ref[j, 528:] = v_ref[:, 128:]


def chunk_product(parts, v):
    return pl.pallas_call(
        chunk_kernel,
        out_shape=[jax.ShapeDtypeStruct((8, 656, 128), F32), jax.ShapeDtypeStruct((128, 256), F32)],
        compiler_params=params(16),
        cost_estimate=cost(3 * 2 * 256 * 256 * 128, 2**22),
    )(parts, v)


def rows_kernel(parts_ref, rows_ref, out_ref):
    total = parts_ref[0, 336:400]
    for j in range(1, 8):
        total = total + parts_ref[j, 336:400]
    for j in range(8):
        out_ref[j, :128] = rows_ref[...]
        out_ref[j, 128:, :128] = total[:32]
        out_ref[j, 128:, 128:] = total[32:]


def rows_pack(parts, rows):
    return pl.pallas_call(
        rows_kernel,
        out_shape=jax.ShapeDtypeStruct((8, 160, 256), F32),
        compiler_params=params(16),
        cost_estimate=cost(2**20, 2**22),
    )(parts, rows)


def turned_three(left, right):
    left_high, left_low = split(left)
    right_high, right_low = split(right)
    dims = (((1,), (1,)), ((), ()))
    return (
        lax.dot_general(left_high, right_high, dims, preferred_element_type=F32)
        + lax.dot_general(left_low, right_high, dims, preferred_element_type=F32)
        + lax.dot_general(left_high, right_low, dims, preferred_element_type=F32)
    )


def pick(core_ref, mine_ref, theirs_ref, run):
    own = pl.program_id(0) // (1024 // WIDE) == core_ref[0]

    @pl.when(own)
    def _():
        run(mine_ref)

    @pl.when(jnp.logical_not(own))
    def _():
        run(theirs_ref)


def first_kernel(core_ref, v1_ref, v2_ref, factor_ref, mine_ref, theirs_ref, base_ref, out_ref, y_ref, wide_ref):
    @pl.when(pl.program_id(0) == 0)
    def _():
        for j in range(4):
            rows = slice(j * 256, j * 256 + 256)
            y = turned_three(jnp.concatenate([v1_ref[rows], v2_ref[rows]], axis=1), factor_ref[...])
            y_ref[rows] = y
            high, low = split(y)
            wide_ref[rows, :256] = high
            wide_ref[rows, 256:] = low

    def run(chunks_ref):
        high, low = split(jnp.concatenate([chunks_ref[j, :256] for j in range(WIDE // 128)], axis=1))
        total = mxu(wide_ref[:, :256], high) + mxu(wide_ref[:, 256:], high) + mxu(wide_ref[:, :256], low)
        out_ref[...] = base_ref[...] + total

    pick(core_ref, mine_ref, theirs_ref, run)


def first_product(core, v1, v2, factor, mine, theirs, base):
    rows, cols = base.shape
    chunks = pl.BlockSpec((WIDE // 128, 656, 128), lambda i, core: (i % (1024 // WIDE), 0, 0))
    block = pl.BlockSpec((rows, WIDE), lambda i, core: (0, i))
    return pl.pallas_call(
        first_kernel,
        grid_spec=pltpu.PrefetchScalarGridSpec(
            num_scalar_prefetch=1,
            grid=(cols // WIDE,),
            in_specs=[pl.BlockSpec((rows, 128), lambda i, core: (0, 0))] * 2
            + [pl.BlockSpec((256, 256), lambda i, core: (0, 0)), chunks, chunks, block],
            out_specs=[block, pl.BlockSpec((rows, 256), lambda i, core: (0, 0))],
            scratch_shapes=[pltpu.VMEM((rows, 512), BF16)],
        ),
        out_shape=[jax.ShapeDtypeStruct((rows, cols), F32), jax.ShapeDtypeStruct((rows, 256), F32)],
        compiler_params=params(58),
        cost_estimate=cost(3 * 2 * rows * cols * 256, 8 * rows * cols),
    )(core, v1, v2, factor, mine, theirs, base)


def last_kernel(core_ref, y_ref, p_ref, gram_ref, factor_ref, mine_ref, theirs_ref, base_ref, out_ref, wide_ref):
    @pl.when(pl.program_id(0) == 0)
    def _():
        gram_high, gram_low = split(gram_ref[...].reshape(256, 256))
        for j in range(8):
            rows = slice(j * 128, j * 128 + 128)
            y_high, y_low = split(y_ref[rows])
            left = p_ref[j, :128] + (mxu(y_high, gram_high) + mxu(y_low, gram_high) + mxu(y_high, gram_low))
            high, low = split(left)
            wide_ref[rows, :256] = high
            wide_ref[rows, 256:] = low

    def run(chunks_ref):
        v = [
            jnp.concatenate([chunks_ref[j, 400:528], chunks_ref[j, 528:]], axis=1) for j in range(WIDE // 128)
        ]
        high, low = split(turned_three(factor_ref[...], jnp.concatenate(v, axis=0)))
        total = mxu(wide_ref[:, :256], high) + mxu(wide_ref[:, 256:], high) + mxu(wide_ref[:, :256], low)
        out_ref[...] = base_ref[...] - total

    pick(core_ref, mine_ref, theirs_ref, run)


def last_product(core, y, p, gram, factor, mine, theirs, base):
    rows, cols = base.shape
    chunks = pl.BlockSpec((WIDE // 128, 656, 128), lambda i, core: (i % (1024 // WIDE), 0, 0))
    block = pl.BlockSpec((rows, WIDE), lambda i, core: (0, i))
    return pl.pallas_call(
        last_kernel,
        grid_spec=pltpu.PrefetchScalarGridSpec(
            num_scalar_prefetch=1,
            grid=(cols // WIDE,),
            in_specs=[
                pl.BlockSpec((rows, 256), lambda i, core: (0, 0)),
                pl.BlockSpec((8, 160, 256), lambda i, core: (0, 0, 0)),
                pl.BlockSpec((8, 32, 256), lambda i, core: (0, 0, 0)),
                pl.BlockSpec((256, 256), lambda i, core: (0, 0)),
                chunks,
                chunks,
                block,
            ],
            out_specs=block,
            scratch_shapes=[pltpu.VMEM((rows, 512), BF16)],
        ),
        out_shape=jax.ShapeDtypeStruct((rows, cols), F32),
        compiler_params=params(58),
        cost_estimate=cost(3 * 2 * rows * cols * 256, 8 * rows * cols),
    )(core, y, p, gram, factor, mine, theirs, base)


def back_kernel(core_ref, v1_ref, v2_ref, factor_ref, mine_ref, theirs_ref, vectors_ref, out_ref, sums_ref):
    def place(ref, half):
        for j in range(8):
            for block in range(4):
                rows = slice(half * 128 + j * 16, half * 128 + j * 16 + 16)
                sums_ref[rows, block * 128 : block * 128 + 128] = ref[j, 256 + 16 * block : 272 + 16 * block]

    @pl.when(core_ref[0] == 0)
    def _():
        place(mine_ref, 0)
        place(theirs_ref, 1)

    @pl.when(core_ref[0] == 1)
    def _():
        place(mine_ref, 1)
        place(theirs_ref, 0)

    mixed = three(factor_ref[...], sums_ref[...])
    out_ref[...] = vectors_ref[...] - three(v1_ref[...], mixed[:128]) - three(v2_ref[...], mixed[128:])


def back_product(core, v1, v2, factor, mine, theirs, vectors):
    return pl.pallas_call(
        back_kernel,
        in_specs=[pl.BlockSpec(memory_space=pltpu.SMEM)] + [pl.BlockSpec(memory_space=pltpu.VMEM)] * 6,
        out_shape=jax.ShapeDtypeStruct(vectors.shape, F32),
        scratch_shapes=[pltpu.VMEM((256, 512), F32)],
        compiler_params=params(16),
        cost_estimate=cost(3 * 2 * 1280 * 256 * 512, 2**23),
    )(core, v1, v2, factor, mine, theirs, vectors)


def shards(matrix, v1, f1, v2, f2, vectors):
    core = lax.axis_index("row") % 2
    col = lax.axis_index("col")

    v_chunk = jnp.concatenate(
        [lax.dynamic_slice_in_dim(v1, col * 128, 128, 0), lax.dynamic_slice_in_dim(v2, col * 128, 128, 0)], axis=1
    )
    v_chunk = lax.ppermute(v_chunk, BOTH, turn_map())

    away, both = away_product((1 - core)[None], v1, v2, matrix)
    came = row_swap(away, 1)
    side_away, side_kept = side_products(core[None], both, v2, vectors)
    side_came = row_swap(side_away, 1)
    kept = kept_product(core[None], both, matrix)

    packed = pack(kept, came, side_kept, side_came)
    packed, v_chunk = lax.optimization_barrier((packed, v_chunk))
    parts = exchange(packed, "row", SAME_CORE)

    packed, over = chunk_product(parts, v_chunk)
    got = exchange(packed, "row", SAME_CORE)
    over = lax.ppermute(over, BOTH, turn_map())
    got, over = lax.optimization_barrier((got, over))

    p_rows = exchange(rows_pack(got, over), "col", None)

    theirs = row_swap(got, 1)
    cross = got[:, 320:336].reshape(128, 128)
    a_right = -small(small(f1, cross), f2)
    factor = jnp.concatenate(
        [jnp.concatenate([f1, a_right], axis=1), jnp.concatenate([jnp.zeros_like(f2), f2], axis=1)], axis=0
    )
    back = back_product(core[None], v1, v2, factor, got, theirs, vectors)
    inner, y_rows = first_product(core[None], v1, v2, factor, got, theirs, matrix)
    p_rows, inner, back = lax.optimization_barrier((p_rows, inner, back))

    gram = p_rows[:, 128:].sum(0)
    gram = gram + row_swap(gram, 1)
    gram = exchange(copies(gram, 8), "row", SAME_CORE)

    updated = last_product(core[None], y_rows, p_rows, gram, factor, got, theirs, inner)
    return updated, back


def solution(mesh):
    in_specs = (P("row", "col"), P("row", None), P(), P("row", None), P(), P("row", "col"))
    out_specs = (P("row", "col"), P("row", "col"))
    return jax.shard_map(shards, mesh=mesh, in_specs=in_specs, out_specs=out_specs, check_vma=False)
```

```python
import jax
import jax.numpy as jnp
from jax import lax
from jax.experimental import pallas as pl
from jax.experimental.pallas import tpu as pltpu
from jax.sharding import PartitionSpec as P

HIGH = lax.Precision.HIGH
BOTH = ("row", "col")
SAME_CORE = [[2 * i + k for i in range(8)] for k in range(2)]
F32 = jnp.float32
BF16 = jnp.bfloat16
WIDE = 512


def dot(left, right, dims=((1,), (0,)), precision=HIGH):
    return lax.dot_general(left, right, (dims, ((), ())), precision=precision, preferred_element_type=F32)


def small(left, right, dims=((1,), (0,))):
    return dot(left, right, dims, lax.Precision.HIGHEST)


def split(value):
    high = value.astype(BF16)
    return high, (value - high.astype(F32)).astype(BF16)


def mxu(left, right):
    return jnp.dot(left, right, preferred_element_type=F32)


def three(left, right):
    left_high, left_low = split(left)
    right_high, right_low = split(right)
    return mxu(left_high, right_high) + mxu(left_low, right_high) + mxu(left_high, right_low)


def row_swap(value, mask):
    return lax.ppermute(value, "row", [(i, i ^ mask) for i in range(16)])


def turn_map():
    return [((2 * j + k) * 8 + c, (2 * c + k) * 8 + j) for j in range(8) for k in range(2) for c in range(8)]


def exchange(value, axis, groups):
    return lax.all_to_all(value, axis, 0, 0, axis_index_groups=groups, tiled=True)


def copies(value, times):
    return jnp.broadcast_to(value[None], (times,) + value.shape)


def params(mebibytes):
    return pltpu.CompilerParams(vmem_limit_bytes=mebibytes * 2**20)


def cost(flops, bytes_accessed):
    return pl.CostEstimate(flops=flops, bytes_accessed=bytes_accessed, transcendentals=0)


def chunk_products(both_ref, matrix_ref, out_ref):
    high, low = split(matrix_ref[...])
    first = mxu(both_ref[...], high)
    total = -(first[:256] + first[256:] + mxu(both_ref[:256], low))
    for side in range(total.shape[1] // 128):
        out_ref[side] = total[:, side * 128 : side * 128 + 128]


def away_kernel(which_ref, v1_ref, v2_ref, matrix_ref, out_ref, both_ref):
    @pl.when(pl.program_id(0) == 0)
    def _():
        high, low = split(v1_ref[...].T)
        both_ref[0:128] = high
        both_ref[256:384] = low
        high, low = split(v2_ref[...].T)
        both_ref[128:256] = high
        both_ref[384:512] = low

    chunk_products(both_ref, matrix_ref, out_ref)


def kept_kernel(which_ref, both_ref, matrix_ref, out_ref):
    chunk_products(both_ref, matrix_ref, out_ref)


def half_product(kernel, which, sides, side_specs, matrix, more_shapes, more_specs):
    depth = matrix.shape[0]
    return pl.pallas_call(
        kernel,
        grid_spec=pltpu.PrefetchScalarGridSpec(
            num_scalar_prefetch=1,
            grid=(1024 // WIDE,),
            in_specs=side_specs
            + [pl.BlockSpec((depth, WIDE), lambda i, which: (0, which[0] * (1024 // WIDE) + i))],
            out_specs=[pl.BlockSpec((WIDE // 128, 256, 128), lambda i, which: (i, 0, 0))] + more_specs,
        ),
        out_shape=[jax.ShapeDtypeStruct((8, 256, 128), F32)] + more_shapes,
        compiler_params=params(58),
        cost_estimate=cost(3 * 2 * 256 * depth * 1024, 4 * depth * 1024 + 2**21),
    )(which, *sides, matrix)


def away_product(which, v1, v2, matrix):
    depth = matrix.shape[0]
    return half_product(
        away_kernel,
        which,
        (v1, v2),
        [pl.BlockSpec((depth, 128), lambda i, which: (0, 0))] * 2,
        matrix,
        [jax.ShapeDtypeStruct((512, depth), BF16)],
        [pl.BlockSpec((512, depth), lambda i, which: (0, 0))],
    )


def kept_product(which, both, matrix):
    depth = matrix.shape[0]
    spec = pl.BlockSpec((512, depth), lambda i, which: (0, 0))
    return half_product(kept_kernel, which, (both,), [spec], matrix, [], [])[0]


def side_kernel(core_ref, both_ref, v2_ref, vectors_ref, away_ref, kept_ref, sums_ref):
    high, low = split(vectors_ref[...])
    sums_ref[...] = mxu(both_ref[:256], high) + mxu(both_ref[256:], high) + mxu(both_ref[:256], low)
    high, low = split(v2_ref[...])
    cross = mxu(both_ref[:128], high) + mxu(both_ref[256:384], high) + mxu(both_ref[:128], low)
    for out_ref, half in ((kept_ref, core_ref[0]), (away_ref, 1 - core_ref[0])):
        for j in range(8):
            rows = pl.ds(pl.multiple_of(half * 128 + j * 16, 16), 16)
            for block in range(4):
                out_ref[j, 16 * block : 16 * block + 16] = sums_ref[rows, block * 128 : block * 128 + 128]
            out_ref[j, 64:] = cross[j * 16 : j * 16 + 16]


def side_products(core, both, v2, vectors):
    return pl.pallas_call(
        side_kernel,
        in_specs=[pl.BlockSpec(memory_space=pltpu.SMEM)] + [pl.BlockSpec(memory_space=pltpu.VMEM)] * 3,
        out_shape=[jax.ShapeDtypeStruct((8, 80, 128), F32)] * 2,
        scratch_shapes=[pltpu.VMEM((256, 512), F32)],
        compiler_params=params(16),
        cost_estimate=cost(3 * 2 * 256 * 1024 * 640, 2**22),
    )(core, both, v2, vectors)


def pack_kernel(kept_ref, came_ref, side_kept_ref, side_came_ref, out_ref):
    out_ref[:, :256] = kept_ref[...] + came_ref[...]
    out_ref[:, 256:] = side_kept_ref[...] + side_came_ref[...]


def pack(*parts):
    return pl.pallas_call(
        pack_kernel,
        out_shape=jax.ShapeDtypeStruct((8, 336, 128), F32),
        compiler_params=params(16),
        cost_estimate=cost(2**19, 2**22),
    )(*parts)


def chunk_kernel(parts_ref, v_ref, out_ref, rows_ref):
    total = parts_ref[0]
    for j in range(1, 8):
        total = total + parts_ref[j]
    rows_ref[...] = total[:256].T
    gram = three(total[:256], v_ref[...])
    for j in range(8):
        out_ref[j, :256] = total[:256]
        out_ref[j, 256:384] = v_ref[:, :128]
        out_ref[j, 384:512] = v_ref[:, 128:]
        out_ref[j, 512:576] = total[256:320]
        out_ref[j, 576:608] = gram[j * 32 : j * 32 + 32, :128]
        out_ref[j, 608:640] = gram[j * 32 : j * 32 + 32, 128:]
        out_ref[j, 640:] = total[320:]


def chunk_product(parts, v):
    return pl.pallas_call(
        chunk_kernel,
        out_shape=[jax.ShapeDtypeStruct((8, 656, 128), F32), jax.ShapeDtypeStruct((128, 256), F32)],
        compiler_params=params(16),
        cost_estimate=cost(3 * 2 * 256 * 256 * 128, 2**22),
    )(parts, v)


def rows_kernel(parts_ref, rows_ref, out_ref):
    total = parts_ref[0]
    for j in range(1, 8):
        total = total + parts_ref[j]
    for j in range(8):
        out_ref[j, :128] = rows_ref[...]
        out_ref[j, 128:, :128] = total[:32]
        out_ref[j, 128:, 128:] = total[32:]


def rows_pack(parts, rows):
    return pl.pallas_call(
        rows_kernel,
        grid=(1,),
        in_specs=[pl.BlockSpec((8, 64, 128), lambda i: (0, 9, 0)), pl.BlockSpec((128, 256), lambda i: (0, 0))],
        out_specs=pl.BlockSpec((8, 160, 256), lambda i: (0, 0, 0)),
        out_shape=jax.ShapeDtypeStruct((8, 160, 256), F32),
        compiler_params=params(16),
        cost_estimate=cost(2**20, 2**22),
    )(parts, rows)


def turned_three(left, right):
    left_high, left_low = split(left)
    right_high, right_low = split(right)
    dims = (((1,), (1,)), ((), ()))
    return (
        lax.dot_general(left_high, right_high, dims, preferred_element_type=F32)
        + lax.dot_general(left_low, right_high, dims, preferred_element_type=F32)
        + lax.dot_general(left_high, right_low, dims, preferred_element_type=F32)
    )


def pick(mine_ref, theirs_ref, run):
    own = pl.program_id(0) < 1024 // WIDE

    @pl.when(own)
    def _():
        run(mine_ref)

    @pl.when(jnp.logical_not(own))
    def _():
        run(theirs_ref)


def half_specs(rows, part):
    steps = 1024 // WIDE
    return (
        pl.BlockSpec((rows, WIDE), lambda i, core: (0, (core[0] * steps + i) % (2 * steps))),
        pl.BlockSpec((WIDE // 128, 256, 128), lambda i, core: (jnp.minimum(i, steps - 1), part, 0)),
        pl.BlockSpec((WIDE // 128, 256, 128), lambda i, core: (jnp.maximum(i - steps, 0), part, 0)),
    )


def first_kernel(core_ref, v1_ref, v2_ref, factor_ref, mine_ref, theirs_ref, base_ref, out_ref, y_ref, wide_ref):
    @pl.when(pl.program_id(0) == 0)
    def _():
        for j in range(4):
            rows = slice(j * 256, j * 256 + 256)
            y = turned_three(jnp.concatenate([v1_ref[rows], v2_ref[rows]], axis=1), factor_ref[...])
            y_ref[rows] = y
            high, low = split(y)
            wide_ref[rows, :256] = high
            wide_ref[rows, 256:] = low

    def run(chunks_ref):
        high, low = split(jnp.concatenate([chunks_ref[j] for j in range(WIDE // 128)], axis=1))
        total = mxu(wide_ref[:, :256], high) + mxu(wide_ref[:, 256:], high) + mxu(wide_ref[:, :256], low)
        out_ref[...] = base_ref[...] + total

    pick(mine_ref, theirs_ref, run)


def first_product(core, v1, v2, factor, mine, theirs, base):
    rows, cols = base.shape
    block, mine_part, theirs_part = half_specs(rows, 0)
    return pl.pallas_call(
        first_kernel,
        grid_spec=pltpu.PrefetchScalarGridSpec(
            num_scalar_prefetch=1,
            grid=(cols // WIDE,),
            in_specs=[pl.BlockSpec((rows, 128), lambda i, core: (0, 0))] * 2
            + [pl.BlockSpec((256, 256), lambda i, core: (0, 0)), mine_part, theirs_part, block],
            out_specs=[block, pl.BlockSpec((rows, 256), lambda i, core: (0, 0))],
            scratch_shapes=[pltpu.VMEM((rows, 512), BF16)],
        ),
        out_shape=[jax.ShapeDtypeStruct((rows, cols), F32), jax.ShapeDtypeStruct((rows, 256), F32)],
        compiler_params=params(58),
        cost_estimate=cost(3 * 2 * rows * cols * 256, 8 * rows * cols),
    )(core, v1, v2, factor, mine, theirs, base)


def last_kernel(core_ref, y_ref, p_ref, gram_ref, factor_ref, mine_ref, theirs_ref, base_ref, out_ref, wide_ref):
    @pl.when(pl.program_id(0) == 0)
    def _():
        gram_high, gram_low = split(gram_ref[...].reshape(256, 256))
        for j in range(8):
            rows = slice(j * 128, j * 128 + 128)
            y_high, y_low = split(y_ref[rows])
            left = p_ref[j, :128] + (mxu(y_high, gram_high) + mxu(y_low, gram_high) + mxu(y_high, gram_low))
            high, low = split(left)
            wide_ref[rows, :256] = high
            wide_ref[rows, 256:] = low

    def run(chunks_ref):
        v = [
            jnp.concatenate([chunks_ref[j, :128], chunks_ref[j, 128:]], axis=1) for j in range(WIDE // 128)
        ]
        high, low = split(turned_three(factor_ref[...], jnp.concatenate(v, axis=0)))
        total = mxu(wide_ref[:, :256], high) + mxu(wide_ref[:, 256:], high) + mxu(wide_ref[:, :256], low)
        out_ref[...] = base_ref[...] - total

    pick(mine_ref, theirs_ref, run)


def last_product(core, y, p, gram, factor, mine, theirs, base):
    rows, cols = base.shape
    block, mine_part, theirs_part = half_specs(rows, 1)
    return pl.pallas_call(
        last_kernel,
        grid_spec=pltpu.PrefetchScalarGridSpec(
            num_scalar_prefetch=1,
            grid=(cols // WIDE,),
            in_specs=[
                pl.BlockSpec((rows, 256), lambda i, core: (0, 0)),
                pl.BlockSpec((8, 160, 256), lambda i, core: (0, 0, 0)),
                pl.BlockSpec((8, 32, 256), lambda i, core: (0, 0, 0)),
                pl.BlockSpec((256, 256), lambda i, core: (0, 0)),
                mine_part,
                theirs_part,
                block,
            ],
            out_specs=block,
            scratch_shapes=[pltpu.VMEM((rows, 512), BF16)],
        ),
        out_shape=jax.ShapeDtypeStruct((rows, cols), F32),
        compiler_params=params(58),
        cost_estimate=cost(3 * 2 * rows * cols * 256, 8 * rows * cols),
    )(core, y, p, gram, factor, mine, theirs, base)


def back_kernel(core_ref, v1_ref, v2_ref, factor_ref, mine_ref, theirs_ref, vectors_ref, out_ref, sums_ref):
    def place(ref, half):
        for j in range(8):
            for block in range(4):
                rows = slice(half * 128 + j * 16, half * 128 + j * 16 + 16)
                sums_ref[rows, block * 128 : block * 128 + 128] = ref[j, 16 * block : 16 * block + 16]

    @pl.when(core_ref[0] == 0)
    def _():
        place(mine_ref, 0)
        place(theirs_ref, 1)

    @pl.when(core_ref[0] == 1)
    def _():
        place(mine_ref, 1)
        place(theirs_ref, 0)

    mixed = three(factor_ref[...], sums_ref[...])
    out_ref[...] = vectors_ref[...] - three(v1_ref[...], mixed[:128]) - three(v2_ref[...], mixed[128:])


def back_product(core, v1, v2, factor, mine, theirs, vectors):
    rows = vectors.shape[0]
    whole = lambda height, width: pl.BlockSpec((height, width), lambda i, core: (0, 0))
    part = pl.BlockSpec((8, 64, 128), lambda i, core: (0, 8, 0))
    return pl.pallas_call(
        back_kernel,
        grid_spec=pltpu.PrefetchScalarGridSpec(
            num_scalar_prefetch=1,
            grid=(1,),
            in_specs=[whole(rows, 128), whole(rows, 128), whole(256, 256), part, part, whole(rows, 512)],
            out_specs=whole(rows, 512),
            scratch_shapes=[pltpu.VMEM((256, 512), F32)],
        ),
        out_shape=jax.ShapeDtypeStruct(vectors.shape, F32),
        compiler_params=params(24),
        cost_estimate=cost(3 * 2 * 1280 * 256 * 512, 2**23),
    )(core, v1, v2, factor, mine, theirs, vectors)


def shards(matrix, v1, f1, v2, f2, vectors):
    core = lax.axis_index("row") % 2
    col = lax.axis_index("col")

    v_chunk = jnp.concatenate(
        [lax.dynamic_slice_in_dim(v1, col * 128, 128, 0), lax.dynamic_slice_in_dim(v2, col * 128, 128, 0)], axis=1
    )
    v_chunk = lax.ppermute(v_chunk, BOTH, turn_map())

    away, both = away_product((1 - core)[None], v1, v2, matrix)
    came = row_swap(away, 1)
    side_away, side_kept = side_products(core[None], both, v2, vectors)
    side_came = row_swap(side_away, 1)
    kept = kept_product(core[None], both, matrix)

    packed = pack(kept, came, side_kept, side_came)
    packed, v_chunk = lax.optimization_barrier((packed, v_chunk))
    parts = exchange(packed, "row", SAME_CORE)

    packed, over = chunk_product(parts, v_chunk)
    got = exchange(packed, "row", SAME_CORE)
    over = lax.ppermute(over, BOTH, turn_map())
    got, over = lax.optimization_barrier((got, over))

    p_rows = exchange(rows_pack(got, over), "col", None)

    theirs = row_swap(got, 1)
    cross = got[:, 640:].reshape(128, 128)
    a_right = -small(small(f1, cross), f2)
    factor = jnp.concatenate(
        [jnp.concatenate([f1, a_right], axis=1), jnp.concatenate([jnp.zeros_like(f2), f2], axis=1)], axis=0
    )
    back = back_product(core[None], v1, v2, factor, got, theirs, vectors)
    inner, y_rows = first_product(core[None], v1, v2, factor, got, theirs, matrix)
    p_rows, inner = lax.optimization_barrier((p_rows, inner))

    gram = p_rows[:, 128:].sum(0)
    gram = gram + row_swap(gram, 1)
    gram = exchange(copies(gram, 8), "row", SAME_CORE)

    gram, back = lax.optimization_barrier((gram, back))
    updated = last_product(core[None], y_rows, p_rows, gram, factor, got, theirs, inner)
    return updated, back


def solution(mesh):
    in_specs = (P("row", "col"), P("row", None), P(), P("row", None), P(), P("row", "col"))
    out_specs = (P("row", "col"), P("row", "col"))
    return jax.shard_map(shards, mesh=mesh, in_specs=in_specs, out_specs=out_specs, check_vma=False)
```

```python
import jax
import jax.numpy as jnp
from jax import lax
from jax.experimental import pallas as pl
from jax.experimental.pallas import tpu as pltpu
from jax.sharding import PartitionSpec as P

HIGH = lax.Precision.HIGH
BOTH = ("row", "col")
SAME_CORE = [[2 * i + k for i in range(8)] for k in range(2)]
F32 = jnp.float32
BF16 = jnp.bfloat16
WIDE = 512


def dot(left, right, dims=((1,), (0,)), precision=HIGH):
    return lax.dot_general(left, right, (dims, ((), ())), precision=precision, preferred_element_type=F32)


def small(left, right, dims=((1,), (0,))):
    return dot(left, right, dims, lax.Precision.HIGHEST)


def split(value):
    high = value.astype(BF16)
    return high, (value - high.astype(F32)).astype(BF16)


def mxu(left, right):
    return jnp.dot(left, right, preferred_element_type=F32)


def three(left, right):
    left_high, left_low = split(left)
    right_high, right_low = split(right)
    return mxu(left_high, right_high) + mxu(left_low, right_high) + mxu(left_high, right_low)


def row_swap(value, mask):
    return lax.ppermute(value, "row", [(i, i ^ mask) for i in range(16)])


def turn_map():
    return [((2 * j + k) * 8 + c, (2 * c + k) * 8 + j) for j in range(8) for k in range(2) for c in range(8)]


def exchange(value, axis, groups):
    return lax.all_to_all(value, axis, 0, 0, axis_index_groups=groups, tiled=True)


def copies(value, times):
    return jnp.broadcast_to(value[None], (times,) + value.shape)


def params(mebibytes):
    return pltpu.CompilerParams(vmem_limit_bytes=mebibytes * 2**20)


def cost(flops, bytes_accessed):
    return pl.CostEstimate(flops=flops, bytes_accessed=bytes_accessed, transcendentals=0)


def chunk_products(both_ref, matrix_ref, out_ref):
    high, low = split(matrix_ref[...])
    first = mxu(both_ref[...], high)
    total = -(first[:256] + first[256:] + mxu(both_ref[:256], low))
    for side in range(total.shape[1] // 128):
        out_ref[side] = total[:, side * 128 : side * 128 + 128]


def away_kernel(which_ref, v1_ref, v2_ref, matrix_ref, out_ref, both_ref):
    @pl.when(pl.program_id(0) == 0)
    def _():
        high, low = split(v1_ref[...].T)
        both_ref[0:128] = high
        both_ref[256:384] = low
        high, low = split(v2_ref[...].T)
        both_ref[128:256] = high
        both_ref[384:512] = low

    chunk_products(both_ref, matrix_ref, out_ref)


def kept_kernel(which_ref, both_ref, matrix_ref, out_ref):
    chunk_products(both_ref, matrix_ref, out_ref)


def half_product(kernel, which, sides, side_specs, matrix, more_shapes, more_specs):
    depth = matrix.shape[0]
    return pl.pallas_call(
        kernel,
        grid_spec=pltpu.PrefetchScalarGridSpec(
            num_scalar_prefetch=1,
            grid=(1024 // WIDE,),
            in_specs=side_specs
            + [pl.BlockSpec((depth, WIDE), lambda i, which: (0, which[0] * (1024 // WIDE) + i))],
            out_specs=[pl.BlockSpec((WIDE // 128, 256, 128), lambda i, which: (i, 0, 0))] + more_specs,
        ),
        out_shape=[jax.ShapeDtypeStruct((8, 256, 128), F32)] + more_shapes,
        compiler_params=params(58),
        cost_estimate=cost(3 * 2 * 256 * depth * 1024, 4 * depth * 1024 + 2**21),
    )(which, *sides, matrix)


def away_product(which, v1, v2, matrix):
    depth = matrix.shape[0]
    return half_product(
        away_kernel,
        which,
        (v1, v2),
        [pl.BlockSpec((depth, 128), lambda i, which: (0, 0))] * 2,
        matrix,
        [jax.ShapeDtypeStruct((512, depth), BF16)],
        [pl.BlockSpec((512, depth), lambda i, which: (0, 0))],
    )


def kept_product(which, both, matrix):
    depth = matrix.shape[0]
    spec = pl.BlockSpec((512, depth), lambda i, which: (0, 0))
    return half_product(kept_kernel, which, (both,), [spec], matrix, [], [])[0]


def side_kernel(core_ref, both_ref, v2_ref, vectors_ref, away_ref, kept_ref, sums_ref):
    high, low = split(vectors_ref[...])
    sums_ref[...] = mxu(both_ref[:256], high) + mxu(both_ref[256:], high) + mxu(both_ref[:256], low)
    high, low = split(v2_ref[...])
    cross = mxu(both_ref[:128], high) + mxu(both_ref[256:384], high) + mxu(both_ref[:128], low)
    for out_ref, half in ((kept_ref, core_ref[0]), (away_ref, 1 - core_ref[0])):
        for j in range(8):
            rows = pl.ds(pl.multiple_of(half * 128 + j * 16, 16), 16)
            for block in range(4):
                out_ref[j, 16 * block : 16 * block + 16] = sums_ref[rows, block * 128 : block * 128 + 128]
            out_ref[j, 64:] = cross[j * 16 : j * 16 + 16]


def side_products(core, both, v2, vectors):
    return pl.pallas_call(
        side_kernel,
        in_specs=[pl.BlockSpec(memory_space=pltpu.SMEM)] + [pl.BlockSpec(memory_space=pltpu.VMEM)] * 3,
        out_shape=[jax.ShapeDtypeStruct((8, 80, 128), F32)] * 2,
        scratch_shapes=[pltpu.VMEM((256, 512), F32)],
        compiler_params=params(16),
        cost_estimate=cost(3 * 2 * 256 * 1024 * 640, 2**22),
    )(core, both, v2, vectors)


def pack_kernel(kept_ref, came_ref, side_kept_ref, side_came_ref, out_ref):
    out_ref[:, :256] = kept_ref[...] + came_ref[...]
    out_ref[:, 256:] = side_kept_ref[...] + side_came_ref[...]


def pack(*parts):
    return pl.pallas_call(
        pack_kernel,
        out_shape=jax.ShapeDtypeStruct((8, 336, 128), F32),
        compiler_params=params(16),
        cost_estimate=cost(2**19, 2**22),
    )(*parts)


def chunk_kernel(parts_ref, v_ref, out_ref, rows_ref):
    total = parts_ref[0]
    for j in range(1, 8):
        total = total + parts_ref[j]
    rows_ref[...] = total[:256].T
    for j in range(8):
        out_ref[j, :256] = total[:256]
        out_ref[j, 256:384] = v_ref[:, :128]
        out_ref[j, 384:512] = v_ref[:, 128:]
        out_ref[j, 512:] = total[256:]


def chunk_product(parts, v):
    return pl.pallas_call(
        chunk_kernel,
        out_shape=[jax.ShapeDtypeStruct((8, 592, 128), F32), jax.ShapeDtypeStruct((128, 256), F32)],
        compiler_params=params(16),
        cost_estimate=cost(2**20, 2**22),
    )(parts, v)


def rows_kernel(chip_ref, p_ref, v_ref, rows_ref, out_ref):
    total = jnp.zeros((32, 256), F32)
    for j in range(8):
        total = total + three(p_ref[j], jnp.concatenate([v_ref[j, :128], v_ref[j, 128:]], axis=1))
    for j in range(8):
        out_ref[j, :128] = rows_ref[...]
        out_ref[j, 128:] = total


def rows_pack(chip, parts, rows):
    return pl.pallas_call(
        rows_kernel,
        grid_spec=pltpu.PrefetchScalarGridSpec(
            num_scalar_prefetch=1,
            grid=(1,),
            in_specs=[
                pl.BlockSpec((8, 32, 128), lambda i, chip: (0, chip[0], 0)),
                pl.BlockSpec((8, 256, 128), lambda i, chip: (0, 1, 0)),
                pl.BlockSpec((128, 256), lambda i, chip: (0, 0)),
            ],
            out_specs=pl.BlockSpec((8, 160, 256), lambda i, chip: (0, 0, 0)),
        ),
        out_shape=jax.ShapeDtypeStruct((8, 160, 256), F32),
        compiler_params=params(16),
        cost_estimate=cost(3 * 2 * 32 * 1024 * 256, 2**22),
    )(chip, parts, parts, rows)


def turned_three(left, right):
    left_high, left_low = split(left)
    right_high, right_low = split(right)
    dims = (((1,), (1,)), ((), ()))
    return (
        lax.dot_general(left_high, right_high, dims, preferred_element_type=F32)
        + lax.dot_general(left_low, right_high, dims, preferred_element_type=F32)
        + lax.dot_general(left_high, right_low, dims, preferred_element_type=F32)
    )


def pick(mine_ref, theirs_ref, run):
    own = pl.program_id(0) < 1024 // WIDE

    @pl.when(own)
    def _():
        run(mine_ref)

    @pl.when(jnp.logical_not(own))
    def _():
        run(theirs_ref)


def half_specs(rows, part):
    steps = 1024 // WIDE
    return (
        pl.BlockSpec((rows, WIDE), lambda i, core: (0, (core[0] * steps + i) % (2 * steps))),
        pl.BlockSpec((WIDE // 128, 256, 128), lambda i, core: (jnp.minimum(i, steps - 1), part, 0)),
        pl.BlockSpec((WIDE // 128, 256, 128), lambda i, core: (jnp.maximum(i - steps, 0), part, 0)),
    )


def first_kernel(core_ref, v1_ref, v2_ref, factor_ref, mine_ref, theirs_ref, base_ref, out_ref, y_ref, wide_ref):
    @pl.when(pl.program_id(0) == 0)
    def _():
        for j in range(4):
            rows = slice(j * 256, j * 256 + 256)
            y = turned_three(jnp.concatenate([v1_ref[rows], v2_ref[rows]], axis=1), factor_ref[...])
            y_ref[rows] = y
            high, low = split(y)
            wide_ref[rows, :256] = high
            wide_ref[rows, 256:] = low

    def run(chunks_ref):
        high, low = split(jnp.concatenate([chunks_ref[j] for j in range(WIDE // 128)], axis=1))
        total = mxu(wide_ref[:, :256], high) + mxu(wide_ref[:, 256:], high) + mxu(wide_ref[:, :256], low)
        out_ref[...] = base_ref[...] + total

    pick(mine_ref, theirs_ref, run)


def first_product(core, v1, v2, factor, mine, theirs, base):
    rows, cols = base.shape
    block, mine_part, theirs_part = half_specs(rows, 0)
    return pl.pallas_call(
        first_kernel,
        grid_spec=pltpu.PrefetchScalarGridSpec(
            num_scalar_prefetch=1,
            grid=(cols // WIDE,),
            in_specs=[pl.BlockSpec((rows, 128), lambda i, core: (0, 0))] * 2
            + [pl.BlockSpec((256, 256), lambda i, core: (0, 0)), mine_part, theirs_part, block],
            out_specs=[block, pl.BlockSpec((rows, 256), lambda i, core: (0, 0))],
            scratch_shapes=[pltpu.VMEM((rows, 512), BF16)],
        ),
        out_shape=[jax.ShapeDtypeStruct((rows, cols), F32), jax.ShapeDtypeStruct((rows, 256), F32)],
        compiler_params=params(58),
        cost_estimate=cost(3 * 2 * rows * cols * 256, 8 * rows * cols),
    )(core, v1, v2, factor, mine, theirs, base)


def last_kernel(core_ref, y_ref, p_ref, gram_ref, factor_ref, mine_ref, theirs_ref, base_ref, out_ref, wide_ref):
    @pl.when(pl.program_id(0) == 0)
    def _():
        gram_high, gram_low = split(gram_ref[...].reshape(256, 256))
        for j in range(8):
            rows = slice(j * 128, j * 128 + 128)
            y_high, y_low = split(y_ref[rows])
            left = p_ref[j, :128] + (mxu(y_high, gram_high) + mxu(y_low, gram_high) + mxu(y_high, gram_low))
            high, low = split(left)
            wide_ref[rows, :256] = high
            wide_ref[rows, 256:] = low

    def run(chunks_ref):
        v = [
            jnp.concatenate([chunks_ref[j, :128], chunks_ref[j, 128:]], axis=1) for j in range(WIDE // 128)
        ]
        high, low = split(turned_three(factor_ref[...], jnp.concatenate(v, axis=0)))
        total = mxu(wide_ref[:, :256], high) + mxu(wide_ref[:, 256:], high) + mxu(wide_ref[:, :256], low)
        out_ref[...] = base_ref[...] - total

    pick(mine_ref, theirs_ref, run)


def last_product(core, y, p, gram, factor, mine, theirs, base):
    rows, cols = base.shape
    block, mine_part, theirs_part = half_specs(rows, 1)
    return pl.pallas_call(
        last_kernel,
        grid_spec=pltpu.PrefetchScalarGridSpec(
            num_scalar_prefetch=1,
            grid=(cols // WIDE,),
            in_specs=[
                pl.BlockSpec((rows, 256), lambda i, core: (0, 0)),
                pl.BlockSpec((8, 160, 256), lambda i, core: (0, 0, 0)),
                pl.BlockSpec((8, 32, 256), lambda i, core: (0, 0, 0)),
                pl.BlockSpec((256, 256), lambda i, core: (0, 0)),
                mine_part,
                theirs_part,
                block,
            ],
            out_specs=block,
            scratch_shapes=[pltpu.VMEM((rows, 512), BF16)],
        ),
        out_shape=jax.ShapeDtypeStruct((rows, cols), F32),
        compiler_params=params(58),
        cost_estimate=cost(3 * 2 * rows * cols * 256, 8 * rows * cols),
    )(core, y, p, gram, factor, mine, theirs, base)


def back_kernel(core_ref, v1_ref, v2_ref, factor_ref, mine_ref, theirs_ref, vectors_ref, out_ref, sums_ref):
    def place(ref, half):
        for j in range(8):
            for block in range(4):
                rows = slice(half * 128 + j * 16, half * 128 + j * 16 + 16)
                sums_ref[rows, block * 128 : block * 128 + 128] = ref[j, 16 * block : 16 * block + 16]

    @pl.when(core_ref[0] == 0)
    def _():
        place(mine_ref, 0)
        place(theirs_ref, 1)

    @pl.when(core_ref[0] == 1)
    def _():
        place(mine_ref, 1)
        place(theirs_ref, 0)

    mixed = three(factor_ref[...], sums_ref[...])
    out_ref[...] = vectors_ref[...] - three(v1_ref[...], mixed[:128]) - three(v2_ref[...], mixed[128:])


def back_product(core, v1, v2, factor, mine, theirs, vectors):
    rows = vectors.shape[0]
    whole = lambda height, width: pl.BlockSpec((height, width), lambda i, core: (0, 0))
    part = pl.BlockSpec((8, 64, 128), lambda i, core: (0, 8, 0))
    return pl.pallas_call(
        back_kernel,
        grid_spec=pltpu.PrefetchScalarGridSpec(
            num_scalar_prefetch=1,
            grid=(1,),
            in_specs=[whole(rows, 128), whole(rows, 128), whole(256, 256), part, part, whole(rows, 512)],
            out_specs=whole(rows, 512),
            scratch_shapes=[pltpu.VMEM((256, 512), F32)],
        ),
        out_shape=jax.ShapeDtypeStruct(vectors.shape, F32),
        compiler_params=params(24),
        cost_estimate=cost(3 * 2 * 1280 * 256 * 512, 2**23),
    )(core, v1, v2, factor, mine, theirs, vectors)


def shards(matrix, v1, f1, v2, f2, vectors):
    core = lax.axis_index("row") % 2
    chip = lax.axis_index("row") // 2
    col = lax.axis_index("col")

    v_chunk = jnp.concatenate(
        [lax.dynamic_slice_in_dim(v1, col * 128, 128, 0), lax.dynamic_slice_in_dim(v2, col * 128, 128, 0)], axis=1
    )
    v_chunk = lax.ppermute(v_chunk, BOTH, turn_map())

    away, both = away_product((1 - core)[None], v1, v2, matrix)
    came = row_swap(away, 1)
    side_away, side_kept = side_products(core[None], both, v2, vectors)
    side_came = row_swap(side_away, 1)
    kept = kept_product(core[None], both, matrix)

    packed = pack(kept, came, side_kept, side_came)
    packed, v_chunk = lax.optimization_barrier((packed, v_chunk))
    parts = exchange(packed, "row", SAME_CORE)

    packed, over = chunk_product(parts, v_chunk)
    got = exchange(packed, "row", SAME_CORE)
    over = lax.ppermute(over, BOTH, turn_map())
    got, over = lax.optimization_barrier((got, over))

    p_rows = exchange(rows_pack(chip[None], got, over), "col", None)

    theirs = row_swap(got, 1)
    cross = got[:, 576:].reshape(128, 128)
    a_right = -small(small(f1, cross), f2)
    factor = jnp.concatenate(
        [jnp.concatenate([f1, a_right], axis=1), jnp.concatenate([jnp.zeros_like(f2), f2], axis=1)], axis=0
    )
    back = back_product(core[None], v1, v2, factor, got, theirs, vectors)
    inner, y_rows = first_product(core[None], v1, v2, factor, got, theirs, matrix)
    p_rows, inner = lax.optimization_barrier((p_rows, inner))

    gram = p_rows[:, 128:].sum(0)
    gram = gram + row_swap(gram, 1)
    gram = exchange(copies(gram, 8), "row", SAME_CORE)

    gram, back = lax.optimization_barrier((gram, back))
    updated = last_product(core[None], y_rows, p_rows, gram, factor, got, theirs, inner)
    return updated, back


def solution(mesh):
    in_specs = (P("row", "col"), P("row", None), P(), P("row", None), P(), P("row", "col"))
    out_specs = (P("row", "col"), P("row", "col"))
    return jax.shard_map(shards, mesh=mesh, in_specs=in_specs, out_specs=out_specs, check_vma=False)
```

```python
import jax
import jax.numpy as jnp
from jax import lax
from jax.experimental import pallas as pl
from jax.experimental.pallas import tpu as pltpu
from jax.sharding import PartitionSpec as P

HIGH = lax.Precision.HIGH
BOTH = ("row", "col")
SAME_CORE = [[2 * i + k for i in range(8)] for k in range(2)]
F32 = jnp.float32
BF16 = jnp.bfloat16
WIDE = 512


def dot(left, right, dims=((1,), (0,)), precision=HIGH):
    return lax.dot_general(left, right, (dims, ((), ())), precision=precision, preferred_element_type=F32)


def small(left, right, dims=((1,), (0,))):
    return dot(left, right, dims, lax.Precision.HIGHEST)


def split(value):
    high = value.astype(BF16)
    return high, (value - high.astype(F32)).astype(BF16)


def mxu(left, right):
    return jnp.dot(left, right, preferred_element_type=F32)


def three(left, right):
    left_high, left_low = split(left)
    right_high, right_low = split(right)
    return mxu(left_high, right_high) + mxu(left_low, right_high) + mxu(left_high, right_low)


def row_swap(value, mask):
    return lax.ppermute(value, "row", [(i, i ^ mask) for i in range(16)])


def turn_map():
    return [((2 * j + k) * 8 + c, (2 * c + k) * 8 + j) for j in range(8) for k in range(2) for c in range(8)]


def exchange(value, axis, groups):
    return lax.all_to_all(value, axis, 0, 0, axis_index_groups=groups, tiled=True)


def copies(value, times):
    return jnp.broadcast_to(value[None], (times,) + value.shape)


def params(mebibytes):
    return pltpu.CompilerParams(vmem_limit_bytes=mebibytes * 2**20)


def cost(flops, bytes_accessed):
    return pl.CostEstimate(flops=flops, bytes_accessed=bytes_accessed, transcendentals=0)


def chunk_products(both_ref, matrix_ref, out_ref):
    high, low = split(matrix_ref[...])
    first = mxu(both_ref[...], high)
    total = -(first[:256] + first[256:] + mxu(both_ref[:256], low))
    for side in range(total.shape[1] // 128):
        out_ref[side] = total[:, side * 128 : side * 128 + 128]


def away_kernel(which_ref, v1_ref, v2_ref, matrix_ref, out_ref, both_ref):
    @pl.when(pl.program_id(0) == 0)
    def _():
        high, low = split(v1_ref[...].T)
        both_ref[0:128] = high
        both_ref[256:384] = low
        high, low = split(v2_ref[...].T)
        both_ref[128:256] = high
        both_ref[384:512] = low

    chunk_products(both_ref, matrix_ref, out_ref)


def kept_kernel(which_ref, both_ref, matrix_ref, out_ref):
    chunk_products(both_ref, matrix_ref, out_ref)


def half_product(kernel, which, sides, side_specs, matrix, more_shapes, more_specs):
    depth = matrix.shape[0]
    return pl.pallas_call(
        kernel,
        grid_spec=pltpu.PrefetchScalarGridSpec(
            num_scalar_prefetch=1,
            grid=(1024 // WIDE,),
            in_specs=side_specs
            + [pl.BlockSpec((depth, WIDE), lambda i, which: (0, which[0] * (1024 // WIDE) + i))],
            out_specs=[pl.BlockSpec((WIDE // 128, 256, 128), lambda i, which: (i, 0, 0))] + more_specs,
        ),
        out_shape=[jax.ShapeDtypeStruct((8, 256, 128), F32)] + more_shapes,
        compiler_params=params(58),
        cost_estimate=cost(3 * 2 * 256 * depth * 1024, 4 * depth * 1024 + 2**21),
    )(which, *sides, matrix)


def away_product(which, v1, v2, matrix):
    depth = matrix.shape[0]
    return half_product(
        away_kernel,
        which,
        (v1, v2),
        [pl.BlockSpec((depth, 128), lambda i, which: (0, 0))] * 2,
        matrix,
        [jax.ShapeDtypeStruct((512, depth), BF16)],
        [pl.BlockSpec((512, depth), lambda i, which: (0, 0))],
    )


def kept_product(which, both, matrix):
    depth = matrix.shape[0]
    spec = pl.BlockSpec((512, depth), lambda i, which: (0, 0))
    return half_product(kept_kernel, which, (both,), [spec], matrix, [], [])[0]


def side_kernel(core_ref, both_ref, v2_ref, vectors_ref, away_ref, kept_ref, sums_ref):
    high, low = split(vectors_ref[...])
    sums_ref[...] = mxu(both_ref[:256], high) + mxu(both_ref[256:], high) + mxu(both_ref[:256], low)
    high, low = split(v2_ref[...])
    cross = mxu(both_ref[:128], high) + mxu(both_ref[256:384], high) + mxu(both_ref[:128], low)
    for out_ref, half in ((kept_ref, core_ref[0]), (away_ref, 1 - core_ref[0])):
        for j in range(8):
            rows = pl.ds(pl.multiple_of(half * 128 + j * 16, 16), 16)
            for block in range(4):
                out_ref[j, 16 * block : 16 * block + 16] = sums_ref[rows, block * 128 : block * 128 + 128]
            out_ref[j, 64:] = cross[j * 16 : j * 16 + 16]


def side_products(core, both, v2, vectors):
    return pl.pallas_call(
        side_kernel,
        in_specs=[pl.BlockSpec(memory_space=pltpu.SMEM)] + [pl.BlockSpec(memory_space=pltpu.VMEM)] * 3,
        out_shape=[jax.ShapeDtypeStruct((8, 80, 128), F32)] * 2,
        scratch_shapes=[pltpu.VMEM((256, 512), F32)],
        compiler_params=params(16),
        cost_estimate=cost(3 * 2 * 256 * 1024 * 640, 2**22),
    )(core, both, v2, vectors)


def pack_kernel(kept_ref, came_ref, side_kept_ref, side_came_ref, out_ref):
    out_ref[:, :256] = kept_ref[...] + came_ref[...]
    out_ref[:, 256:] = side_kept_ref[...] + side_came_ref[...]


def pack(*parts):
    return pl.pallas_call(
        pack_kernel,
        out_shape=jax.ShapeDtypeStruct((8, 336, 128), F32),
        compiler_params=params(16),
        cost_estimate=cost(2**19, 2**22),
    )(*parts)


def chunk_kernel(parts_ref, v_ref, out_ref, rows_ref):
    total = parts_ref[0]
    for j in range(1, 8):
        total = total + parts_ref[j]
    rows_ref[...] = total[:256].T
    for j in range(8):
        out_ref[j, :256] = total[:256]
        out_ref[j, 256:384] = v_ref[:, :128]
        out_ref[j, 384:512] = v_ref[:, 128:]
        out_ref[j, 512:] = total[256:]


def chunk_product(parts, v):
    return pl.pallas_call(
        chunk_kernel,
        out_shape=[jax.ShapeDtypeStruct((8, 592, 128), F32), jax.ShapeDtypeStruct((128, 256), F32)],
        compiler_params=params(16),
        cost_estimate=cost(2**20, 2**22),
    )(parts, v)


def rows_kernel(chip_ref, p_ref, v_ref, rows_ref, out_ref):
    total = jnp.zeros((32, 256), F32)
    for j in range(8):
        total = total + three(p_ref[j], jnp.concatenate([v_ref[j, :128], v_ref[j, 128:]], axis=1))
    for j in range(8):
        out_ref[j, :128] = rows_ref[...]
        out_ref[j, 128:] = total


def rows_pack(chip, parts, rows):
    return pl.pallas_call(
        rows_kernel,
        grid_spec=pltpu.PrefetchScalarGridSpec(
            num_scalar_prefetch=1,
            grid=(1,),
            in_specs=[
                pl.BlockSpec((8, 32, 128), lambda i, chip: (0, chip[0], 0)),
                pl.BlockSpec((8, 256, 128), lambda i, chip: (0, 1, 0)),
                pl.BlockSpec((128, 256), lambda i, chip: (0, 0)),
            ],
            out_specs=pl.BlockSpec((8, 160, 256), lambda i, chip: (0, 0, 0)),
        ),
        out_shape=jax.ShapeDtypeStruct((8, 160, 256), F32),
        compiler_params=params(16),
        cost_estimate=cost(3 * 2 * 32 * 1024 * 256, 2**22),
    )(chip, parts, parts, rows)


def turned_three(left, right):
    left_high, left_low = split(left)
    right_high, right_low = split(right)
    dims = (((1,), (1,)), ((), ()))
    return (
        lax.dot_general(left_high, right_high, dims, preferred_element_type=F32)
        + lax.dot_general(left_low, right_high, dims, preferred_element_type=F32)
        + lax.dot_general(left_high, right_low, dims, preferred_element_type=F32)
    )


def pick(mine_ref, theirs_ref, run):
    own = pl.program_id(0) < 1024 // WIDE

    @pl.when(own)
    def _():
        run(mine_ref)

    @pl.when(jnp.logical_not(own))
    def _():
        run(theirs_ref)


def half_specs(rows, part):
    steps = 1024 // WIDE
    return (
        pl.BlockSpec((rows, WIDE), lambda i, core: (0, (core[0] * steps + i) % (2 * steps))),
        pl.BlockSpec((WIDE // 128, 256, 128), lambda i, core: (jnp.minimum(i, steps - 1), part, 0)),
        pl.BlockSpec((WIDE // 128, 256, 128), lambda i, core: (jnp.maximum(i - steps, 0), part, 0)),
    )


def first_kernel(core_ref, v1_ref, v2_ref, factor_ref, mine_ref, theirs_ref, base_ref, out_ref, y_ref, wide_ref):
    @pl.when(pl.program_id(0) == 0)
    def _():
        for j in range(4):
            rows = slice(j * 256, j * 256 + 256)
            y = turned_three(jnp.concatenate([v1_ref[rows], v2_ref[rows]], axis=1), factor_ref[...])
            y_ref[rows] = y
            high, low = split(y)
            wide_ref[rows, :256] = high
            wide_ref[rows, 256:] = low

    def run(chunks_ref):
        high, low = split(jnp.concatenate([chunks_ref[j] for j in range(WIDE // 128)], axis=1))
        total = mxu(wide_ref[:, :256], high) + mxu(wide_ref[:, 256:], high) + mxu(wide_ref[:, :256], low)
        out_ref[...] = base_ref[...] + total

    pick(mine_ref, theirs_ref, run)


def first_product(core, v1, v2, factor, mine, theirs, base):
    rows, cols = base.shape
    block, mine_part, theirs_part = half_specs(rows, 0)
    return pl.pallas_call(
        first_kernel,
        grid_spec=pltpu.PrefetchScalarGridSpec(
            num_scalar_prefetch=1,
            grid=(cols // WIDE,),
            in_specs=[pl.BlockSpec((rows, 128), lambda i, core: (0, 0))] * 2
            + [pl.BlockSpec((256, 256), lambda i, core: (0, 0)), mine_part, theirs_part, block],
            out_specs=[block, pl.BlockSpec((rows, 256), lambda i, core: (0, 0))],
            scratch_shapes=[pltpu.VMEM((rows, 512), BF16)],
        ),
        out_shape=[jax.ShapeDtypeStruct((rows, cols), F32), jax.ShapeDtypeStruct((rows, 256), F32)],
        compiler_params=params(58),
        cost_estimate=cost(3 * 2 * rows * cols * 256, 8 * rows * cols),
    )(core, v1, v2, factor, mine, theirs, base)


def last_kernel(core_ref, y_ref, p_ref, gram_ref, factor_ref, mine_ref, theirs_ref, base_ref, out_ref, wide_ref):
    @pl.when(pl.program_id(0) == 0)
    def _():
        gram_high, gram_low = split(gram_ref[...].reshape(256, 256))
        for j in range(8):
            rows = slice(j * 128, j * 128 + 128)
            y_high, y_low = split(y_ref[rows])
            left = p_ref[j, :128] + (mxu(y_high, gram_high) + mxu(y_low, gram_high) + mxu(y_high, gram_low))
            high, low = split(left)
            wide_ref[rows, :256] = high
            wide_ref[rows, 256:] = low

    def run(chunks_ref):
        v = [
            jnp.concatenate([chunks_ref[j, :128], chunks_ref[j, 128:]], axis=1) for j in range(WIDE // 128)
        ]
        high, low = split(turned_three(factor_ref[...], jnp.concatenate(v, axis=0)))
        total = mxu(wide_ref[:, :256], high) + mxu(wide_ref[:, 256:], high) + mxu(wide_ref[:, :256], low)
        out_ref[...] = base_ref[...] - total

    pick(mine_ref, theirs_ref, run)


def last_product(core, y, p, gram, factor, mine, theirs, base):
    rows, cols = base.shape
    block, mine_part, theirs_part = half_specs(rows, 1)
    return pl.pallas_call(
        last_kernel,
        grid_spec=pltpu.PrefetchScalarGridSpec(
            num_scalar_prefetch=1,
            grid=(cols // WIDE,),
            in_specs=[
                pl.BlockSpec((rows, 256), lambda i, core: (0, 0)),
                pl.BlockSpec((8, 160, 256), lambda i, core: (0, 0, 0)),
                pl.BlockSpec((8, 32, 256), lambda i, core: (0, 0, 0)),
                pl.BlockSpec((256, 256), lambda i, core: (0, 0)),
                mine_part,
                theirs_part,
                block,
            ],
            out_specs=block,
            scratch_shapes=[pltpu.VMEM((rows, 512), BF16)],
        ),
        out_shape=jax.ShapeDtypeStruct((rows, cols), F32),
        compiler_params=params(58),
        cost_estimate=cost(3 * 2 * rows * cols * 256, 8 * rows * cols),
    )(core, y, p, gram, factor, mine, theirs, base)


def back_kernel(core_ref, v1_ref, v2_ref, factor_ref, mine_ref, theirs_ref, vectors_ref, out_ref, sums_ref):
    def place(ref, half):
        for j in range(8):
            for block in range(4):
                rows = slice(half * 128 + j * 16, half * 128 + j * 16 + 16)
                sums_ref[rows, block * 128 : block * 128 + 128] = ref[j, 16 * block : 16 * block + 16]

    @pl.when(core_ref[0] == 0)
    def _():
        place(mine_ref, 0)
        place(theirs_ref, 1)

    @pl.when(core_ref[0] == 1)
    def _():
        place(mine_ref, 1)
        place(theirs_ref, 0)

    mixed = three(factor_ref[...], sums_ref[...])
    out_ref[...] = vectors_ref[...] - three(v1_ref[...], mixed[:128]) - three(v2_ref[...], mixed[128:])


def back_product(core, v1, v2, factor, mine, theirs, vectors):
    rows = vectors.shape[0]
    whole = lambda height, width: pl.BlockSpec((height, width), lambda i, core: (0, 0))
    part = pl.BlockSpec((8, 64, 128), lambda i, core: (0, 8, 0))
    return pl.pallas_call(
        back_kernel,
        grid_spec=pltpu.PrefetchScalarGridSpec(
            num_scalar_prefetch=1,
            grid=(1,),
            in_specs=[whole(rows, 128), whole(rows, 128), whole(256, 256), part, part, whole(rows, 512)],
            out_specs=whole(rows, 512),
            scratch_shapes=[pltpu.VMEM((256, 512), F32)],
        ),
        out_shape=jax.ShapeDtypeStruct(vectors.shape, F32),
        compiler_params=params(58),
        cost_estimate=cost(3 * 2 * 1280 * 256 * 512, 2**23),
    )(core, v1, v2, factor, mine, theirs, vectors)


def shards(matrix, v1, f1, v2, f2, vectors):
    core = lax.axis_index("row") % 2
    chip = lax.axis_index("row") // 2
    col = lax.axis_index("col")

    v_chunk = jnp.concatenate(
        [lax.dynamic_slice_in_dim(v1, col * 128, 128, 0), lax.dynamic_slice_in_dim(v2, col * 128, 128, 0)], axis=1
    )
    v_chunk = lax.ppermute(v_chunk, BOTH, turn_map())

    away, both = away_product((1 - core)[None], v1, v2, matrix)
    came = row_swap(away, 1)
    side_away, side_kept = side_products(core[None], both, v2, vectors)
    side_came = row_swap(side_away, 1)
    kept = kept_product(core[None], both, matrix)

    packed = pack(kept, came, side_kept, side_came)
    packed, v_chunk = lax.optimization_barrier((packed, v_chunk))
    parts = exchange(packed, "row", SAME_CORE)

    packed, over = chunk_product(parts, v_chunk)
    got = exchange(packed, "row", SAME_CORE)
    over = lax.ppermute(over, BOTH, turn_map())
    got, over = lax.optimization_barrier((got, over))

    p_rows = exchange(rows_pack(chip[None], got, over), "col", None)

    theirs = row_swap(got, 1)
    cross = got[:, 576:].reshape(128, 128)
    a_right = -small(small(f1, cross), f2)
    factor = jnp.concatenate(
        [jnp.concatenate([f1, a_right], axis=1), jnp.concatenate([jnp.zeros_like(f2), f2], axis=1)], axis=0
    )
    back = back_product(core[None], v1, v2, factor, got, theirs, vectors)
    inner, y_rows = first_product(core[None], v1, v2, factor, got, theirs, matrix)
    p_rows, inner = lax.optimization_barrier((p_rows, inner))

    gram = p_rows[:, 128:].sum(0)
    gram = gram + row_swap(gram, 1)
    gram = exchange(copies(gram, 8), "row", SAME_CORE)

    gram, back = lax.optimization_barrier((gram, back))
    updated = last_product(core[None], y_rows, p_rows, gram, factor, got, theirs, inner)
    return updated, back


def solution(mesh):
    in_specs = (P("row", "col"), P("row", None), P(), P("row", None), P(), P("row", "col"))
    out_specs = (P("row", "col"), P("row", "col"))
    return jax.shard_map(shards, mesh=mesh, in_specs=in_specs, out_specs=out_specs, check_vma=False)
```
